256 devices in a mesh: expert: 32 (over x, z), tensor: 8 (over y, core).
Axes of the slice: x: 4, y: 4, z: 8, core: 2. Of those that a mesh axis runs over, the one named last changes fastest.
Arguments:
- attn_partials: bfloat16 [8, 2, 2048, 4096], P('tensor', None, 'expert'), may hold values from -4 to 4
- resid: bfloat16 [2, 2048, 4096], P(None, 'expert'), may hold values from -6 to 6
- norm_gain: float32 [4096], replicated, may hold values from 0.25 to 1.75
- expert_ids: int32 [2, 2048, 8], P(None, 'expert'), may hold values from 0 to 31, all different within a row; in each aligned block of 8 rows (0 to 7, 8 to 15, ..., all dimensions but the last counted through in order) at most 3 rows name the same one
- gate_num: int32 [2, 2048, 8], P(None, 'expert'), may hold values from 1 to 128
- w_gate: bfloat16 [32, 4096, 3072], P('expert', None, 'tensor'), may hold values from -0.09375 to 0.09375
- w_up: bfloat16 [32, 4096, 3072], P('expert', None, 'tensor'), may hold values from -0.09375 to 0.09375
- w_down: bfloat16 [32, 3072, 4096], P('expert', 'tensor'), may hold values from -0.109375 to 0.109375
Outputs:
- residual_out: bfloat16 [2, 2048, 4096], P(None, ('expert', 'tensor'))
- expert_mix: bfloat16 [2, 2048, 4096], P(None, ('expert', 'tensor'))
The draws below stay inside these ranges and needn't reach their ends.
Inputs may be any that keep to these rules, and one draw needn't show every extreme that they name: `expert_ids`: each row names 8 different experts. In each aligned block of 8 rows (the rows of one device, branch 0 first), no expert is named by more than 3 rows, a bound that some block reaches.
All inputs are finite; a program needn't handle non-finite values.
Results may differ from the reference program's by a relative error of at most 0.034.
Values may be sent and summed in bfloat16 or wider, within the bound.
A program may use at most 128 MiB of HBM per device.

```python
import math
import jax
import jax.numpy as jnp
import numpy as np
from jax import lax

D = 4096
FF = 3072
TOP = 8
TOK_DEV = 8
EXPERTS = 32
CAP = 3
TOKENS = 2048
N_TENSOR = 8


def touch_ends(array, stream_key, smallest, high):
    spot = [jax.random.randint(jax.random.fold_in(stream_key, axis), (), 0, length) for axis, length in enumerate(array.shape)]
    main_axis = array.shape.index(max(array.shape))
    beside = spot[:main_axis] + [(spot[main_axis] + 1) % array.shape[main_axis]] + spot[main_axis + 1:]
    return array.at[tuple(spot)].set(smallest).at[tuple(beside)].set(high)


def raised(array, key, source, target, blocks, factor):
    def block_of(axis_at):
        return (jnp.arange(array.shape[axis_at]) // (array.shape[axis_at] // blocks)).reshape((-1,) + (1,) * (array.ndim - 1 - axis_at))

    first = jax.random.permutation(key, blocks)[block_of(target)]
    other_side = (block_of(target) + blocks // 2) % blocks
    return jnp.where((block_of(source) == first) | (block_of(source) == other_side), factor * array, array)


def block_scale(rng, dims, shards, least, top_value):
    gain = 1.0
    for dim, shards_of in shards:
        draws = jax.random.uniform(jax.random.fold_in(jax.random.fold_in(rng, 6), dim), (shards_of,), jnp.float32, least / len(shards), top_value / len(shards))
        gain = gain * jnp.repeat(jnp.exp(draws), dims[dim] // shards_of).reshape((-1,) + (1,) * (len(dims) - 1 - dim))
    return gain


def routed_block(own_key, own, number, rows, count, top, limit, slope):
    order = jax.random.permutation(own_key, count)
    heavy_load, ordinary = portions_of(count, rows * top, limit, slope, True), portions_of(count, rows * top, limit, slope, False)
    places = jnp.arange(count)

    def named(tallies, offset_by):
        used = int((tallies > 0).sum())
        fixed = max(1, used // 4)
        passed = fixed + (places - fixed + offset_by * (used - fixed)) % max(1, count - fixed)
        return jnp.zeros((count,), jnp.int32).at[order[jnp.where(places < fixed, places, passed)]].set(jnp.asarray(tallies, jnp.int32))

    tallies = jnp.where(number % 4 == 0, named(heavy_load, number // 4), named(ordinary, number - number // 4 - 1))
    mixed = jax.random.permutation(jax.random.fold_in(own, 3), count)
    giver, taker = mixed[0:count // 2 * 2:2], mixed[1:count // 2 * 2:2]
    margin = jnp.minimum(tallies[giver] - 1, limit - tallies[taker]) // 2
    margin = jnp.where((giver == order[0]) | (taker == order[0]) | (tallies[taker] == 0), 0, jnp.maximum(margin, 0))
    passed = jax.random.randint(jax.random.fold_in(own, 4), (count // 2,), 0, 1 << 20) % (margin + 1)
    tallies = tallies.at[giver].add(-passed).at[taker].add(passed)
    items = jnp.searchsorted(jnp.cumsum(tallies), jnp.arange(rows * top), side="right").astype(jnp.int32)
    listing = items.reshape(top, rows).T
    listing = listing[jax.random.permutation(jax.random.fold_in(own, 1), rows)]
    offset_by = jax.random.randint(jax.random.fold_in(own, 2), (rows, 1), 0, top)
    return jnp.take_along_axis(listing, (jnp.arange(top)[None, :] + offset_by) % top, axis=1)


def portions_of(amount, total, limit, lean, full):
    loads = [(1 << 20) // math.isqrt(standing ** lean) + 1 for standing in range(1, amount + 1)]
    largest = limit if full else min(limit, max(-(-total // amount), total * loads[0] // sum(loads)))
    least = 1 if total - largest >= amount - 1 else 0
    counts, rest = [largest] + [least] * (amount - 1), total - largest - least * (amount - 1)
    while rest > 0:
        candidates = [i for i in range(1, amount) if counts[i] < largest] or [i for i in range(1, amount) if counts[i] < limit]
        whole, remaining = sum([loads[i] for i in candidates]), rest
        for i in candidates:
            more = min(limit - counts[i], max(1, remaining * loads[i] // whole), rest)
            counts[i] = counts[i] + more
            rest = rest - more
    return np.array(counts)


def normal_values(key, shape, spread, most, pieces=(), kind=jnp.bfloat16):
    level = block_scale(key, shape, pieces, -0.22, 0.18) if pieces else 1.0
    array = jax.random.normal(key, shape, jnp.float32) * spread * level
    return jnp.minimum(jnp.maximum(array, -most), most).astype(kind)


def noise_with(key, extent, deviation, reach, shards, heavy, held_as=jnp.bfloat16):
    result = deviation * jax.random.normal(key, extent, jnp.float32)
    if shards:
        result = result * block_scale(key, extent, shards, -0.22, 0.18)
    return jnp.clip(raised(result, jax.random.fold_in(key, 3), *heavy), -reach, reach).astype(held_as)


def setup_inputs(seed: int = 0) -> dict:
    arg_keys = jax.random.split(jax.random.key(seed), 9)
    attn_partials = noise_with(arg_keys[0], (N_TENSOR, 2, TOKENS, D), 0.5, 4.0, ((0, 8), (2, 32)), (0, 2, 8, 2.0))
    resid = normal_values(arg_keys[1], (2, TOKENS, D), 1.0, 6.0, ((1, 32),))
    norm_gain = jnp.clip(1.0 + 0.15 * jax.random.normal(arg_keys[2], (D,), jnp.float32), 0.25, 1.75)
    expert_ids_keys = jax.random.split(jax.random.fold_in(arg_keys[3], 1), 2 * TOKENS // TOK_DEV)
    expert_ids_turns = jax.random.permutation(jax.random.fold_in(arg_keys[3], 3), 2 * TOKENS // TOK_DEV)
    expert_ids = jax.vmap(lambda own, number: routed_block(jax.random.fold_in(arg_keys[3], 2), own, number, TOK_DEV, EXPERTS, TOP, CAP, 2))(expert_ids_keys, expert_ids_turns).reshape((2, TOKENS, TOP))
    gate_num = touch_ends(jax.random.randint(arg_keys[4], (2, TOKENS, TOP), 1, 129), jax.random.fold_in(arg_keys[4], 1), 1, 128).astype(jnp.int32)
    w_gate = normal_values(arg_keys[5], (EXPERTS, D, FF), D ** -0.5, 0.09375, ((0, 32), (2, 8)))
    w_up = normal_values(arg_keys[6], (EXPERTS, D, FF), D ** -0.5, 0.09375, ((0, 32), (2, 8)))
    w_down = normal_values(arg_keys[7], (EXPERTS, FF, D), FF ** -0.5, 0.109375, ((0, 32), (1, 8)))
    return dict(attn_partials=attn_partials, resid=resid, norm_gain=norm_gain, expert_ids=expert_ids, gate_num=gate_num, w_gate=w_gate, w_up=w_up, w_down=w_down)


def apply_expert(rows, wg, wu, wd):
    gate = jnp.dot(rows, wg, preferred_element_type=jnp.float32)
    up = jnp.dot(rows, wu, preferred_element_type=jnp.float32)
    hidden = (jax.nn.silu(gate) * up).astype(jnp.bfloat16)
    blocks = hidden.reshape(rows.shape[0], N_TENSOR, FF // N_TENSOR).astype(jnp.float32)
    down = wd.reshape(N_TENSOR, FF // N_TENSOR, D).astype(jnp.float32)
    parts = jnp.einsum('rtf,tfd->rtd', blocks, down, precision=lax.Precision.HIGHEST)
    parts = lax.optimization_barrier(parts.astype(jnp.bfloat16)).astype(jnp.float32)
    total = lax.optimization_barrier(jnp.sum(parts, axis=1))
    return lax.optimization_barrier(total.astype(jnp.bfloat16)).astype(jnp.float32)

def reference(attn_partials, resid, norm_gain, expert_ids, gate_num, w_gate, w_up, w_down):
    attn = lax.optimization_barrier(jnp.sum(attn_partials.astype(jnp.float32), axis=0))
    hstate = resid.astype(jnp.float32) + attn
    residual_out = hstate.astype(jnp.bfloat16)
    meansq = lax.optimization_barrier(jnp.mean(hstate * hstate, axis=-1, keepdims=True))
    normed = (hstate * lax.rsqrt(meansq + 1e-06) * norm_gain.astype(jnp.float32)).astype(jnp.bfloat16)
    row_count = 2 * TOKENS
    blocks = row_count // TOK_DEV
    rows = normed.reshape(row_count, D)
    labels = expert_ids.reshape(row_count, TOP)
    weights = gate_num.reshape(row_count, TOP).astype(jnp.float32) / 128.0
    row_ids = jnp.arange(row_count, dtype=jnp.int32)

    def one_expert(total, inputs):
        label, wg, wu, wd = inputs
        hit = labels == label
        member = jnp.any(hit, axis=-1).astype(jnp.int32)
        weight = lax.optimization_barrier(jnp.sum(jnp.where(hit, weights, 0.0), axis=-1))
        grouped = member.reshape(blocks, TOK_DEV)
        rank = (jnp.cumsum(grouped, axis=1) - grouped).astype(jnp.int32)
        slot = (jnp.arange(blocks, dtype=jnp.int32)[:, None] * CAP + rank).reshape(-1)
        slot = jnp.where(member == 1, slot, blocks * CAP).astype(jnp.int32)
        table = jnp.zeros((blocks * CAP,), jnp.int32).at[slot].set(row_ids, mode='drop')
        output = apply_expert(rows[table], wg, wu, wd)
        back = output[jnp.minimum(slot, blocks * CAP - 1)]
        return (total + weight[:, None] * back, None)
    start = jnp.zeros((row_count, D), jnp.float32)
    total, _ = lax.scan(one_expert, start, (jnp.arange(EXPERTS, dtype=jnp.int32), w_gate, w_up, w_down))
    expert_mix = total.reshape(2, TOKENS, D).astype(jnp.bfloat16)
    return (residual_out, expert_mix)
```

```python
import functools

import jax
import jax.numpy as jnp
from jax import lax
from jax.experimental import pallas as pl
from jax.experimental.pallas import tpu as pltpu
from jax.sharding import PartitionSpec as P

MESH = pl.DeviceIdType.MESH
BF16 = jnp.bfloat16
F32 = jnp.float32
BLOCK = 8


def grid_of(experts):
    return (4, experts // 4) if experts >= 4 else (1, experts)


def groups_of(nz):
    if nz == 8:
        return ((0, 1), (4, -2), (3, -3), (2, -1))
    return tuple((dz,) for dz in range(nz))


def kernel(
    cfg,
    attn, resid, gain, ids, nums, wg, wu, wd,
    out_res, out_mix,
    wgu, wdv, ap, arb, atr, afin, rsd, hs, nrm, rsend, rbuf, ssend, sbuf,
    rank, gate, sel, selw, snd, xg, acc, hid, own, sib, rb, tr, fin, back, msend, mbuf,
    lsem, ssem, rsem,
):
    experts, nt, nx, nz, cap, d = cfg
    ny = nt // 2
    dc = d // nt
    tg = attn.shape[0]
    per = tg // nt
    f = wg.shape[1]
    nb = tg // BLOCK
    sl = nb * cap

    e = lax.axis_index("expert")
    t = lax.axis_index("tensor")
    x, z = e // nz, lax.rem(e, nz)
    y, c = t // 2, lax.rem(t, 2)
    step = 1 - 2 * c
    yf = lax.rem(y + step + ny, ny)
    yb = lax.rem(y - step + ny, ny)
    yo = lax.rem(y + 2, ny)
    sibling = (e, y * 2 + 1 - c)
    ahead = (e, yf * 2 + c)
    behind = (e, yb * 2 + c)

    offsets, groups = [], []
    for dzs in groups_of(nz):
        start = len(offsets)
        for dz in dzs:
            for dx in range(nx):
                offsets.append((dx, dz % nz))
        groups.append((start, len(offsets)))

    def expert_at(k, sign=1):
        dx, dz = offsets[k]
        ex = lax.rem(x + (dx if sign > 0 else nx - dx), nx)
        ez = lax.rem(z + (dz if sign > 0 else nz - dz), nz)
        return ex * nz + ez

    counter = {"l": 0, "s": 0, "r": 0}
    sent = []

    def fresh(kind):
        counter[kind] += 1
        return counter[kind] - 1

    def local(src, dst):
        return pltpu.make_async_copy(src, dst, lsem.at[fresh("l")])

    def remote(src, dst, device):
        copy = pltpu.make_async_remote_copy(
            src_ref=src, dst_ref=dst, send_sem=ssem.at[fresh("s")], recv_sem=rsem.at[fresh("r")],
            device_id=device, device_id_type=MESH,
        )
        copy.start()
        sent.append(copy)
        return copy

    barrier = pltpu.get_barrier_semaphore()
    peers = 0
    for k, (dx, dz) in enumerate(offsets):
        if (dx, dz) != (0, 0):
            pl.semaphore_signal(barrier, inc=1, device_id=(expert_at(k), t), device_id_type=MESH)
            peers += 1
    for i in range(1, nt):
        pl.semaphore_signal(barrier, inc=1, device_id=(e, lax.rem(t + i, nt)), device_id_type=MESH)
        peers += 1

    def cols(ref, j):
        return ref.at[:, pl.ds(pl.multiple_of(j * dc, dc), dc)]

    own_loads = [local(cols(attn, 2 * yy + c), ap.at[yy]) for yy in range(ny)]
    own_loads.append(local(cols(resid, t), rsd))
    for copy in own_loads:
        copy.start()
    w_loads = [local(wg, wgu.at[:, pl.ds(0, f)]), local(wu, wgu.at[:, pl.ds(f, f)])]
    for j in range(nt):
        w_loads.append(local(wd.at[:, pl.ds(j * dc, dc)], wdv.at[j]))
    for copy in w_loads:
        copy.start()

    pl.semaphore_wait(barrier, peers)

    a1 = [remote(cols(attn, 2 * yy + 1 - c), arb.at[yy], sibling) for yy in range(ny)]

    lane = lax.broadcasted_iota(jnp.int32, (experts, tg), 0)
    member = jnp.zeros((experts, tg), F32)
    weight = jnp.zeros((experts, tg), F32)
    for k in range(ids.shape[0]):
        hit = ids[k : k + 1, :] == lane
        member = member + jnp.where(hit, 1.0, 0.0)
        weight = weight + jnp.where(hit, nums[k : k + 1, :].astype(F32) / 128.0, 0.0)
    ri = lax.broadcasted_iota(jnp.int32, (tg, tg), 0)
    ci = lax.broadcasted_iota(jnp.int32, (tg, tg), 1)
    lower = jnp.where((ri // BLOCK == ci // BLOCK) & (ri < ci), 1.0, 0.0).astype(BF16)
    before = jnp.dot(member.astype(BF16), lower, preferred_element_type=F32)
    rank[...] = jnp.where(member > 0.5, before, -1.0)
    gate[...] = weight
    ji = lax.broadcasted_iota(jnp.int32, (sl, tg), 0)
    bi = lax.broadcasted_iota(jnp.int32, (sl, tg), 1) // BLOCK
    jd = jnp.zeros((sl, tg), jnp.int32)
    for m in range(1, nb):
        jd = jd + jnp.where(ji >= m * cap, 1, 0)
    want = jnp.where(jd == bi, (ji - jd * cap).astype(F32), -2.0)
    for k in range(experts):
        at = pl.ds(expert_at(k), 1)
        chosen = want == rank[at, :]
        sel[k * sl : (k + 1) * sl, :] = jnp.where(chosen, 1.0, 0.0).astype(BF16)
        selw[k * sl : (k + 1) * sl, :] = jnp.where(chosen, gate[at, :], 0.0).astype(BF16)

    for copy in own_loads:
        copy.wait()
    for copy in a1:
        copy.wait_recv()

    def add_to(ref, i, *others):
        total = ref[i].astype(F32)
        for other in others:
            total = total + other.astype(F32)
        ref[i] = total.astype(BF16)

    add_to(ap, yo, arb[yo])
    a2 = remote(ap.at[yo], atr, ahead)
    add_to(ap, yb, arb[yb])
    a3 = remote(ap.at[yb], afin.at[1], behind)
    add_to(ap, yf, arb[yf])
    a2.wait_recv()
    add_to(ap, yf, atr[...])
    a4 = remote(ap.at[yf], afin.at[0], ahead)
    mine = ap[y].astype(F32) + arb[y].astype(F32) + rsd[...].astype(F32)
    a3.wait_recv()
    mine = mine + afin[1].astype(F32)
    a4.wait_recv()
    mine = mine + afin[0].astype(F32)
    half = tg // 2
    state = jnp.concatenate(
        [
            mine[b * half + i * BLOCK : b * half + (i + 1) * BLOCK]
            for i in range(nt)
            for b in range(2)
        ],
        axis=0,
    )
    hs[...] = state

    part = jnp.sum(state * state, axis=1, keepdims=True)
    ssend[...] = jnp.transpose(jnp.broadcast_to(part, (tg, tg)))[:8]
    sums = []
    for i in range(1, nt):
        sums.append(remote(ssend, sbuf.at[t], (e, lax.rem(t + i, nt))))
    sbuf[t] = ssend[...]
    rsend[...] = state.astype(BF16)

    def to_rows(src, dst):
        copies = []
        for i in range(1, nt):
            to = lax.rem(t + i, nt)
            rows = pl.ds(pl.multiple_of(to * per, per), per)
            copies.append(remote(src.at[rows], dst.at[t], (e, to)))
        keep = local(src.at[pl.ds(pl.multiple_of(t * per, per), per)], dst.at[t])
        keep.start()
        return copies, keep

    for copy in sums:
        copy.wait_recv()
    total = sbuf[0]
    for i in range(1, nt):
        total = total + sbuf[i]
    total = jnp.transpose(jnp.concatenate([total] * (tg // 8), axis=0))
    scale = lax.rsqrt(total * (1.0 / d) + 1e-06)
    mygain = gain[pl.ds(t, 1), :]
    for j in range(dc // tg):
        at = slice(j * tg, (j + 1) * tg)
        nrm[:, at] = (hs[:, at] * scale * mygain[:, at]).astype(BF16)

    there = [None] * experts
    for k0, k1 in groups:
        rows = slice(k0 * sl, k1 * sl)
        snd[rows, :] = jnp.dot(sel[rows, :], nrm[...], preferred_element_type=F32).astype(BF16)
        for k in range(k0, k1):
            at = pl.ds(k * sl, sl)
            if offsets[k] == (0, 0):
                there[k] = local(snd.at[at], xg.at[t, at])
                there[k].start()
            else:
                there[k] = remote(snd.at[at], xg.at[t, at], (expert_at(k), t))
    res_rows = to_rows(rsend, rbuf)

    def arrived(k, copies):
        if offsets[k] == (0, 0):
            copies[k].wait()
        else:
            copies[k].wait_recv()

    state_of = [dict() for _ in groups]

    def span(g):
        k0, k1 = groups[g]
        return k0 * sl, (k1 - k0) * sl

    def gather_first(g):
        s = state_of[g]
        r0, rn = span(g)
        for k in range(*groups[g]):
            arrived(k, there)
        block = xg.at[t, pl.ds(r0, rn)]
        s["b"] = remote(block, block, ahead)
        s["f"] = remote(block, block, behind)
        s["near"] = [remote(block, block, sibling)]

    def gather_second(g):
        s = state_of[g]
        r0, rn = span(g)
        s["b"].wait_recv()
        block = xg.at[yb * 2 + c, pl.ds(r0, rn)]
        s["o"] = remote(block, block, ahead)
        s["near"].append(remote(block, block, sibling))
        s["f"].wait_recv()
        block = xg.at[yf * 2 + c, pl.ds(r0, rn)]
        s["near"].append(remote(block, block, sibling))

    def gather_third(g):
        s = state_of[g]
        r0, rn = span(g)
        s["o"].wait_recv()
        block = xg.at[yo * 2 + c, pl.ds(r0, rn)]
        s["near"].append(remote(block, block, sibling))

    def compute(g):
        s = state_of[g]
        r0, rn = span(g)
        for copy in s["near"]:
            copy.wait_recv()
        if g == 0:
            for copy in w_loads:
                copy.wait()
        at = pl.ds(r0, rn)
        acc[:rn, :] = jnp.zeros((rn, 2 * f), F32)

        @pl.loop(0, nt)
        def _(j):
            w = wgu[pl.ds(pl.multiple_of(j * dc, dc), dc), :]
            acc[:rn, :] += jnp.dot(xg[j, at, :], w, preferred_element_type=F32)

        a = acc[:rn, :f]
        hid[:rn, :] = (a / (1.0 + jnp.exp(-a)) * acc[:rn, f:]).astype(BF16)

        @pl.loop(0, ny)
        def _(yy):
            sib[yy, at, :] = jnp.dot(
                hid[:rn, :], wdv[yy * 2 + 1 - c], preferred_element_type=F32
            ).astype(BF16)

        s["pair"] = remote(sib.at[:, at], rb.at[:, at], sibling)

        @pl.loop(0, ny)
        def _(yy):
            own[yy, at, :] = jnp.dot(
                hid[:rn, :], wdv[yy * 2 + c], preferred_element_type=F32
            ).astype(BF16)

    def reduce_first(g):
        s = state_of[g]
        r0, rn = span(g)
        at = pl.ds(r0, rn)
        s["pair"].wait_recv()

        def pair(i):
            own[i, at, :] = (own[i, at, :].astype(F32) + rb[i, at, :].astype(F32)).astype(BF16)

        pair(yo)
        s["t"] = remote(own.at[yo, at], tr.at[at], ahead)
        pair(yb)
        s["f1"] = remote(own.at[yb, at], fin.at[1, at], behind)
        pair(yf)
        pair(y)

    def reduce_second(g):
        s = state_of[g]
        r0, rn = span(g)
        at = pl.ds(r0, rn)
        s["t"].wait_recv()
        own[yf, at, :] = (own[yf, at, :].astype(F32) + tr[at, :].astype(F32)).astype(BF16)
        s["f0"] = remote(own.at[yf, at], fin.at[0, at], ahead)

    back_copies = [None] * experts

    def reduce_third(g):
        s = state_of[g]
        r0, rn = span(g)
        at = pl.ds(r0, rn)
        s["f1"].wait_recv()
        s["f0"].wait_recv()
        own[y, at, :] = (
            own[y, at, :].astype(F32) + fin[0, at, :].astype(F32) + fin[1, at, :].astype(F32)
        ).astype(BF16)
        for k in range(*groups[g]):
            here = pl.ds(k * sl, sl)
            if offsets[k] == (0, 0):
                back_copies[k] = local(own.at[y, here], back.at[here])
                back_copies[k].start()
            else:
                back_copies[k] = remote(own.at[y, here], back.at[here], (expert_at(k, -1), t))

    n = len(groups)
    gather_first(0)
    gather_second(0)
    if n > 1:
        gather_first(1)
    gather_third(0)
    compute(0)
    for g in range(1, n):
        gather_second(g)
        reduce_first(g - 1)
        gather_third(g)
        if g + 1 < n:
            gather_first(g + 1)
        reduce_second(g - 1)
        if g >= 2:
            reduce_third(g - 2)
        compute(g)
    reduce_first(n - 1)
    if n > 1:
        reduce_third(n - 2)
    reduce_second(n - 1)
    reduce_third(n - 1)

    def to_out(copies, buf, out):
        for copy in copies[0]:
            copy.wait_recv()
        copies[1].wait()
        for j in range(nt):
            out[:, j * dc : (j + 1) * dc] = buf[j]

    to_out(res_rows, rbuf, out_res)

    mixed = jnp.zeros((tg, dc), F32)
    for k0, k1 in groups:
        for k in range(k0, k1):
            arrived(k, back_copies)
        rows = slice(k0 * sl, k1 * sl)
        mixed = mixed + lax.dot_general(
            selw[rows, :], back[rows, :], (((0,), (0,)), ((), ())), preferred_element_type=F32
        )
    msend[...] = mixed.astype(BF16)
    to_out(to_rows(msend, mbuf), mbuf, out_mix)
    for copy in sent:
        copy.wait_send()


def shards(attn_partials, resid, norm_gain, expert_ids, gate_num, w_gate, w_up, w_down):
    experts = lax.axis_size("expert")
    nt = lax.axis_size("tensor")
    nx, nz = grid_of(experts)
    _, two, tokens, d = attn_partials.shape
    top = expert_ids.shape[-1]
    tg = two * tokens
    per = tg // nt
    dc = d // nt
    ny = nt // 2
    f = w_gate.shape[-1]
    cap = min(BLOCK, 3 * BLOCK * top // (2 * experts))
    sl = tg // BLOCK * cap
    rows = experts * sl
    most = max(len(g) for g in groups_of(nz)) * nx * sl
    n_groups = len(groups_of(nz))

    def by_device(a):
        a = a.reshape(two, nt, tokens // nt, top)
        return a.transpose(3, 1, 0, 2).reshape(top, tg)

    n_remote = 4 + 3 + 2 * (experts - 1) + 3 * (nt - 1) + 12 * n_groups + ny
    n_local = ny + 3 + nt + 4
    vmem = pl.BlockSpec(memory_space=pltpu.VMEM)
    hbm = pl.BlockSpec(memory_space=pl.ANY)
    scratch = [
        pltpu.VMEM((d, 2 * f), BF16),
        pltpu.VMEM((nt, f, dc), BF16),
        pltpu.VMEM((ny, tg, dc), BF16),
        pltpu.VMEM((ny, tg, dc), BF16),
        pltpu.VMEM((tg, dc), BF16),
        pltpu.VMEM((2, tg, dc), BF16),
        pltpu.VMEM((tg, dc), BF16),
        pltpu.VMEM((tg, dc), F32),
        pltpu.VMEM((tg, dc), BF16),
        pltpu.VMEM((tg, dc), BF16),
        pltpu.VMEM((nt, per, dc), BF16),
        pltpu.VMEM((8, tg), F32),
        pltpu.VMEM((nt, 8, tg), F32),
        pltpu.VMEM((experts, tg), F32),
        pltpu.VMEM((experts, tg), F32),
        pltpu.VMEM((rows, tg), BF16),
        pltpu.VMEM((rows, tg), BF16),
        pltpu.VMEM((rows, dc), BF16),
        pltpu.VMEM((nt, rows, dc), BF16),
        pltpu.VMEM((most, 2 * f), F32),
        pltpu.VMEM((most, f), BF16),
        pltpu.VMEM((ny, rows, dc), BF16),
        pltpu.VMEM((ny, rows, dc), BF16),
        pltpu.VMEM((ny, rows, dc), BF16),
        pltpu.VMEM((rows, dc), BF16),
        pltpu.VMEM((2, rows, dc), BF16),
        pltpu.VMEM((rows, dc), BF16),
        pltpu.VMEM((tg, dc), BF16),
        pltpu.VMEM((nt, per, dc), BF16),
        pltpu.SemaphoreType.DMA((n_local,)),
        pltpu.SemaphoreType.DMA((n_remote,)),
        pltpu.SemaphoreType.DMA((n_remote,)),
    ]
    res, mix = pl.pallas_call(
        functools.partial(kernel, (experts, nt, nx, nz, cap, d)),
        out_shape=[jax.ShapeDtypeStruct((per, d), BF16)] * 2,
        in_specs=[hbm, hbm, vmem, vmem, vmem, hbm, hbm, hbm],
        out_specs=[vmem, vmem],
        scratch_shapes=scratch,
        compiler_params=pltpu.CompilerParams(
            collective_id=0, has_side_effects=True, vmem_limit_bytes=60 * 1024 * 1024
        ),
        cost_estimate=pl.CostEstimate(
            flops=6 * rows * d * f, bytes_accessed=6 * d * f, transcendentals=rows * f
        ),
    )(
        attn_partials.reshape(tg, d),
        resid.reshape(tg, d),
        norm_gain.reshape(nt, dc),
        by_device(expert_ids),
        by_device(gate_num),
        w_gate.reshape(d, f),
        w_up.reshape(d, f),
        w_down.reshape(f, d),
    )
    return (res.reshape(two, per // two, d), mix.reshape(two, per // two, d))


def solution(mesh):
    placed = (
        P("tensor", None, "expert", None),
        P(None, "expert", None),
        P(),
        P(None, "expert", None),
        P(None, "expert", None),
        P("expert", None, "tensor"),
        P("expert", None, "tensor"),
        P("expert", "tensor", None),
    )
    return jax.shard_map(
        shards,
        mesh=mesh,
        in_specs=placed,
        out_specs=(P(None, ("expert", "tensor"), None), P(None, ("expert", "tensor"), None)),
        check_vma=False,
    )
```

```python
import functools
import re

import jax
import jax.numpy as jnp
from jax import lax
from jax.experimental import pallas as pl
from jax.experimental.pallas import tpu as pltpu
from jax.sharding import PartitionSpec as P

MESH = pl.DeviceIdType.MESH
BF16 = jnp.bfloat16
F32 = jnp.float32
BLOCK = 8


NORMAL = "A3B2A2A4B3A1"
DIRECT = "A0B1"
SCHEDULE = (
    "P5A0P1P4P3D5P2P6D1F5P7D4H5F1P0F4D6D3C5D2H4C6F3Q5",
    "C4D7H1F2Q6H3Q4C7D0H2C3T4Q7F0Q3C2H0T5U4T3Q2C0U5U3",
    "Q0T2C1T0Q1U2U0T1V0U1W3W0W5W4W2W1",
)


def grid_of(experts):
    return (4, experts // 4) if experts >= 4 else (1, experts)


def groups_of(nx, nz):
    def offsets(name):
        far = int(name[1])
        if far in (0, nz - far):
            return [(dx, far) for dx in range(nx)]
        flip = name[0] == "B"
        return [(dx, far if (dx < nx // 2) != flip else nz - far) for dx in range(nx)]

    if nx == 4 and nz == 8:
        return [offsets(a + b) for a, b in zip(NORMAL[::2], NORMAL[1::2])], [
            offsets(a + b) for a, b in zip(DIRECT[::2], DIRECT[1::2])
        ]
    return [[(dx, dz) for dx in range(nx)] for dz in range(1, nz)], [offsets("A0")]


def schedule_of(normal, direct):
    if normal == len(NORMAL) // 2 and direct == len(DIRECT) // 2:
        return [(name, int(g)) for name, g in re.findall("([A-Z])([0-9])", "".join(SCHEDULE))]
    steps = [("A", 0)] + [("P", g) for g in range(normal + direct)]
    for names, groups in (("DFHCQTUW", range(normal)), ("DCQ", range(normal, normal + direct))):
        steps += [(name, g) for name in names for g in groups]
    return steps + [("V", 0)]


def kernel(
    cfg,
    attn, resid, gain, ids, nums, wg, wu, wd,
    outs,
    wgu, wdv, ap, arb, afin, rsd, hs, nall, rsend, rbuf, ssend, sbuf,
    rank, gate, sel, selw, snd, snd4, xg, acc, hid, own, sib, rb, tr, fin, back, back4, msd, mrd, mine4, mix, msend, mbuf,
    lsem, ssem, rsem,
):
    experts, nt, nx, nz, cap, d = cfg
    ny = nt // 2
    dc = d // nt
    tg = attn.shape[0]
    per = tg // nt
    f = wg.shape[1]
    nb = tg // BLOCK
    sl = nb * cap

    e = lax.axis_index("expert")
    t = lax.axis_index("tensor")
    x, z = e // nz, lax.rem(e, nz)
    y, c = t // 2, lax.rem(t, 2)
    step = 1 - 2 * c
    yf = lax.rem(y + step + ny, ny)
    yb = lax.rem(y - step + ny, ny)
    yo = lax.rem(y + 2, ny)
    sibling = (e, y * 2 + 1 - c)
    ahead = (e, yf * 2 + c)
    behind = (e, yb * 2 + c)
    opposite = (e, yo * 2 + c)

    offsets, groups = [], []
    normal, direct = groups_of(nx, nz)
    n = len(normal)
    for members in normal + direct:
        groups.append((len(offsets), len(offsets) + len(members)))
        offsets.extend(members)
    kd = groups[n][0]
    rd0 = kd * sl

    def expert_at(k, sign=1):
        dx, dz = offsets[k]
        ex = lax.rem(x + (dx if sign > 0 else nx - dx), nx)
        ez = lax.rem(z + (dz if sign > 0 else nz - dz), nz)
        return ex * nz + ez

    counter = {"l": 0, "s": 0, "r": 0}
    sent = []

    def fresh(kind):
        counter[kind] += 1
        return counter[kind] - 1

    def local(src, dst):
        return pltpu.make_async_copy(src, dst, lsem.at[fresh("l")])

    def remote(src, dst, device):
        copy = pltpu.make_async_remote_copy(
            src_ref=src, dst_ref=dst, send_sem=ssem.at[fresh("s")], recv_sem=rsem.at[fresh("r")],
            device_id=device, device_id_type=MESH,
        )
        copy.start()
        sent.append(copy)
        return copy

    barrier = pltpu.get_barrier_semaphore()
    peers = 0
    for k, (dx, dz) in enumerate(offsets):
        if (dx, dz) != (0, 0):
            pl.semaphore_signal(barrier, inc=1, device_id=(expert_at(k), t), device_id_type=MESH)
            peers += 1
    for i in range(1, nt):
        pl.semaphore_signal(barrier, inc=1, device_id=(e, lax.rem(t + i, nt)), device_id_type=MESH)
        peers += 1

    def cols(ref, j):
        return ref.at[:, pl.ds(pl.multiple_of(j * dc, dc), dc)]

    own_loads = [local(cols(attn, 2 * yy + c), ap.at[yy]) for yy in (yo, yb, yf, y)]
    own_loads.append(local(cols(resid, t), rsd))
    for copy in own_loads:
        copy.start()
    w_loads = [local(wg, wgu.at[:, pl.ds(0, f)]), local(wu, wgu.at[:, pl.ds(f, f)])]
    for j in range(nt):
        w_loads.append(local(wd.at[:, pl.ds(j * dc, dc)], wdv.at[j]))
    for copy in w_loads:
        copy.start()

    pl.semaphore_wait(barrier, peers)

    a1 = [remote(cols(attn, 2 * yy + 1 - c), arb.at[yy], sibling) for yy in (yo, yf, yb, y)]

    half = tg // 2
    ri = lax.broadcasted_iota(jnp.int32, (tg, tg), 0)
    ci = lax.broadcasted_iota(jnp.int32, (tg, tg), 1)
    branch = lax.rem(ci // BLOCK, 2)
    place = branch * half + ci // (2 * BLOCK) * BLOCK + lax.rem(ci, BLOCK)
    order = jnp.where(ri == place, 1.0, 0.0).astype(BF16)

    def by_device(ref):
        return sum(
            jnp.dot(
                ref[b].astype(F32).astype(BF16),
                order[b * half : (b + 1) * half],
                preferred_element_type=F32,
            )
            for b in range(2)
        )

    names, amounts = by_device(ids), by_device(nums)
    lane = lax.broadcasted_iota(jnp.int32, (experts, tg), 0).astype(F32)
    member = jnp.zeros((experts, tg), F32)
    weight = jnp.zeros((experts, tg), F32)
    for k in range(ids.shape[1]):
        hit = names[k : k + 1, :] == lane
        member = member + jnp.where(hit, 1.0, 0.0)
        weight = weight + jnp.where(hit, amounts[k : k + 1, :] * (1.0 / 128.0), 0.0)
    lower = jnp.where((ri // BLOCK == ci // BLOCK) & (ri < ci), 1.0, 0.0).astype(BF16)
    before = jnp.dot(member.astype(BF16), lower, preferred_element_type=F32)
    rank[...] = jnp.where(member > 0.5, before, -1.0)
    gate[...] = weight
    ji = lax.broadcasted_iota(jnp.int32, (sl, tg), 0)
    bi = lax.broadcasted_iota(jnp.int32, (sl, tg), 1) // BLOCK
    jd = jnp.zeros((sl, tg), jnp.int32)
    for m in range(1, nb):
        jd = jd + jnp.where(ji >= m * cap, 1, 0)
    want = jnp.where(jd == bi, (ji - jd * cap).astype(F32), -2.0)
    for k in range(experts):
        at = pl.ds(expert_at(k), 1)
        chosen = want == rank[at, :]
        sel[k * sl : (k + 1) * sl, :] = jnp.where(chosen, 1.0, 0.0).astype(BF16)
        selw[k * sl : (k + 1) * sl, :] = jnp.where(chosen, gate[at, :], 0.0).astype(BF16)

    a2 = []
    for i, (yy, peer) in enumerate(((yo, opposite), (yb, behind), (yf, ahead))):
        own_loads[i].wait()
        a1[i].wait_recv()
        ap[yy] = ap[yy] + arb[yy]
        a2.append(remote(ap.at[yy], afin.at[i], peer))
    for copy in own_loads[3:]:
        copy.wait()
    a1[3].wait_recv()
    mine = ap[y].astype(F32) + arb[y].astype(F32) + rsd[...].astype(F32)
    for i, copy in enumerate(a2):
        copy.wait_recv()
        mine = mine + afin[i].astype(F32)
    state = jnp.concatenate(
        [
            mine[b * half + i * BLOCK : b * half + (i + 1) * BLOCK]
            for i in range(nt)
            for b in range(2)
        ],
        axis=0,
    )
    hs[...] = state

    part = jnp.sum(state * state, axis=1, keepdims=True)
    ssend[...] = jnp.transpose(jnp.broadcast_to(part, (tg, tg)))[:8]
    sums = []
    for i in range(1, nt):
        sums.append(remote(ssend, sbuf.at[t], (e, lax.rem(t + i, nt))))
    sbuf[t] = ssend[...]
    rsend[...] = state.astype(BF16)

    def to_rows(src, dst):
        copies = []
        for i in range(1, nt):
            to = lax.rem(t + i, nt)
            rows = pl.ds(pl.multiple_of(to * per, per), per)
            copies.append(remote(src.at[rows], dst.at[t], (e, to)))
        keep = local(src.at[pl.ds(pl.multiple_of(t * per, per), per)], dst.at[t])
        keep.start()
        return copies, keep

    res_rows = to_rows(rsend, rbuf)
    for copy in sums:
        copy.wait_recv()
    total = sbuf[0]
    for i in range(1, nt):
        total = total + sbuf[i]
    total = jnp.transpose(jnp.concatenate([total] * (tg // 8), axis=0))
    scale = lax.rsqrt(total * (1.0 / d) + 1e-06)
    mygain = gain[:, pl.ds(pl.multiple_of(t * dc, dc), dc)]
    for j in range(dc // tg):
        at = slice(j * tg, (j + 1) * tg)
        nall[y, :, at] = (hs[:, at] * scale * mygain[:, at]).astype(BF16)

    there = [None] * experts

    spread = []

    def spread_rows(g):
        for peer in (opposite, behind, ahead):
            spread.append(remote(nall.at[y], nall.at[y], peer))

    def move(k, src, dst, device):
        if offsets[k] == (0, 0):
            copy = local(src, dst)
            copy.start()
            return copy
        return remote(src, dst, device)

    def dispatch(g):
        k0, k1 = groups[g]
        rows = slice(k0 * sl, k1 * sl)
        if g < n:
            snd[rows, :] = jnp.dot(sel[rows, :], nall[y], preferred_element_type=F32).astype(BF16)
        else:
            if g == n:
                for copy in spread:
                    copy.wait_recv()
            held = slice(k0 * sl - rd0, k1 * sl - rd0)
            for yy in range(ny):
                snd4[yy, held, :] = jnp.dot(
                    sel[rows, :], nall[yy], preferred_element_type=F32
                ).astype(BF16)
        for k in range(k0, k1):
            at = pl.ds(k * sl, sl)
            if g < n:
                there[k] = move(k, snd.at[at], xg.at[c, y, at], (expert_at(k), t))
            else:
                held = pl.ds(k * sl - rd0, sl)
                there[k] = move(k, snd4.at[:, held], xg.at[c, :, at], (expert_at(k), t))

    def arrived(k, copies):
        if offsets[k] == (0, 0):
            copies[k].wait()
        else:
            copies[k].wait_recv()

    state_of = [dict() for _ in groups]

    def span(g):
        k0, k1 = groups[g]
        return k0 * sl, (k1 - k0) * sl

    def gather_first(g):
        s = state_of[g]
        r0, rn = span(g)
        for k in range(*groups[g]):
            arrived(k, there)
        if g >= n:
            block = xg.at[c, :, pl.ds(r0, rn)]
            s["near"] = [remote(block, block, sibling)]
            return
        block = xg.at[c, y, pl.ds(r0, rn)]
        s["b"] = remote(block, block, ahead)
        s["f"] = remote(block, block, behind)
        s["near"] = [remote(block, block, sibling)]

    def gather_second(g):
        s = state_of[g]
        r0, rn = span(g)
        s["b"].wait_recv()
        block = xg.at[c, yb, pl.ds(r0, rn)]
        s["o"] = remote(block, block, ahead)
        s["near"].append(remote(block, block, sibling))
        s["f"].wait_recv()
        block = xg.at[c, yf, pl.ds(r0, rn)]
        s["near"].append(remote(block, block, sibling))

    def gather_third(g):
        s = state_of[g]
        r0, rn = span(g)
        s["o"].wait_recv()
        block = xg.at[c, yo, pl.ds(r0, rn)]
        s["near"].append(remote(block, block, sibling))

    weights_here = []

    def compute(g):
        s = state_of[g]
        r0, rn = span(g)
        for copy in s["near"]:
            copy.wait_recv()
        if not weights_here:
            weights_here.append(True)
            for copy in w_loads:
                copy.wait()
        at = pl.ds(r0, rn)
        acc[:rn, :] = jnp.zeros((rn, 2 * f), F32)

        @pl.loop(0, nt)
        def _(j):
            w = wgu[pl.ds(pl.multiple_of(j * dc, dc), dc), :]
            acc[:rn, :] += jnp.dot(
                xg[lax.rem(j, 2), j // 2, at, :], w, preferred_element_type=F32
            )

        a = acc[:rn, :f]
        hid[:rn, :] = (a / (1.0 + jnp.exp(-a)) * acc[:rn, f:]).astype(BF16)

        @pl.loop(0, ny)
        def _(yy):
            sib[yy, at, :] = jnp.dot(
                hid[:rn, :], wdv[yy * 2 + 1 - c], preferred_element_type=F32
            ).astype(BF16)

        s["pair"] = remote(sib.at[:, at], rb.at[:, at], sibling)

        @pl.loop(0, ny)
        def _(yy):
            own[yy, at, :] = jnp.dot(
                hid[:rn, :], wdv[yy * 2 + c], preferred_element_type=F32
            ).astype(BF16)

    back_copies = [None] * experts

    def reduce_first(g):
        s = state_of[g]
        r0, rn = span(g)
        at = pl.ds(r0, rn)
        s["pair"].wait_recv()

        def pair(i):
            own[i, at, :] = own[i, at, :] + rb[i, at, :]

        if g >= n:
            for i in range(ny):
                pair(i)
            for k in range(*groups[g]):
                here = pl.ds(k * sl, sl)
                held = pl.ds(k * sl - rd0, sl)
                back_copies[k] = move(
                    k, own.at[:, here], back4.at[:, held], (expert_at(k, -1), t)
                )
            return
        pair(yo)
        s["t"] = remote(own.at[yo, at], tr.at[at], ahead)
        pair(yb)
        s["f1"] = remote(own.at[yb, at], fin.at[1, at], behind)
        pair(yf)
        pair(y)

    def reduce_second(g):
        s = state_of[g]
        r0, rn = span(g)
        at = pl.ds(r0, rn)
        s["t"].wait_recv()
        own[yf, at, :] = own[yf, at, :] + tr[at, :]
        s["f0"] = remote(own.at[yf, at], fin.at[0, at], ahead)

    def reduce_third(g):
        s = state_of[g]
        r0, rn = span(g)
        at = pl.ds(r0, rn)
        s["f1"].wait_recv()
        s["f0"].wait_recv()
        own[y, at, :] = (
            own[y, at, :].astype(F32) + fin[0, at, :].astype(F32) + fin[1, at, :].astype(F32)
        ).astype(BF16)
        for k in range(*groups[g]):
            here = pl.ds(k * sl, sl)
            back_copies[k] = move(k, own.at[y, here], back.at[here], (expert_at(k, -1), t))

    def combine(rows, values):
        return lax.dot_general(
            selw[rows, :], values, (((0,), (0,)), ((), ())), preferred_element_type=F32
        )

    summed = []

    def combine_direct(g):
        for k in range(kd, experts):
            arrived(k, back_copies)
        rows = slice(rd0, experts * sl)
        for i, (yy, peer) in enumerate(((yo, opposite), (yb, behind), (yf, ahead))):
            msd[i] = combine(rows, back4[yy]).astype(BF16)
            summed.append(remote(msd.at[i], mrd.at[i], peer))
        mine4[...] = combine(rows, back4[y])

    mixed_groups = []

    def combine_normal(g):
        for k in range(*groups[g]):
            arrived(k, back_copies)
        r0, rn = span(g)
        rows = slice(r0, r0 + rn)
        if mixed_groups:
            mix[...] += combine(rows, back[rows, :])
        else:
            mix[...] = combine(rows, back[rows, :])
        mixed_groups.append(g)

    def to_out(copies, buf, out):
        for copy in copies[0]:
            copy.wait_recv()
        copies[1].wait()
        for j in range(nt):
            out[:, j * dc : (j + 1) * dc] = buf[j]

    def residual_out(g):
        to_out(res_rows, rbuf, outs.at[0])

    steps = dict(
        P=dispatch, D=gather_first, F=gather_second, H=gather_third, C=compute,
        Q=reduce_first, T=reduce_second, U=reduce_third, A=spread_rows, V=combine_direct,
        W=combine_normal,
    )
    for name, g in schedule_of(n, len(direct)):
        steps[name](g)
        if name == "V":
            residual_out(g)

    mixed = mine4[...] + mix[...]
    for i, copy in enumerate(summed):
        copy.wait_recv()
        mixed = mixed + mrd[i].astype(F32)
    msend[...] = mixed.astype(BF16)
    done = list(sent)
    last = to_rows(msend, mbuf)
    for copy in done:
        copy.wait_send()
    to_out(last, mbuf, outs.at[1])
    for copy in sent[len(done) :]:
        copy.wait_send()


def shards(attn_partials, resid, norm_gain, expert_ids, gate_num, w_gate, w_up, w_down):
    experts = lax.axis_size("expert")
    nt = lax.axis_size("tensor")
    nx, nz = grid_of(experts)
    _, two, tokens, d = attn_partials.shape
    top = expert_ids.shape[-1]
    tg = two * tokens
    per = tg // nt
    dc = d // nt
    ny = nt // 2
    f = w_gate.shape[-1]
    cap = min(BLOCK, 3 * BLOCK * top // (2 * experts))
    sl = tg // BLOCK * cap
    rows = experts * sl
    normal, direct = groups_of(nx, nz)
    most = max(len(g) for g in normal + direct) * sl
    nrows = sum(len(g) for g in normal) * sl
    n_groups = len(normal + direct)

    n_remote = 4 + 3 + 2 * (experts - 1) + 3 * (nt - 1) + 12 * n_groups + ny + 8
    n_local = ny + 3 + nt + 4
    vmem = pl.BlockSpec(memory_space=pltpu.VMEM)
    hbm = pl.BlockSpec(memory_space=pl.ANY)
    scratch = [
        pltpu.VMEM((d, 2 * f), BF16),
        pltpu.VMEM((nt, f, dc), BF16),
        pltpu.VMEM((ny, tg, dc), BF16),
        pltpu.VMEM((ny, tg, dc), BF16),
        pltpu.VMEM((3, tg, dc), BF16),
        pltpu.VMEM((tg, dc), BF16),
        pltpu.VMEM((tg, dc), F32),
        pltpu.VMEM((ny, tg, dc), BF16),
        pltpu.VMEM((tg, dc), BF16),
        pltpu.VMEM((nt, per, dc), BF16),
        pltpu.VMEM((8, tg), F32),
        pltpu.VMEM((nt, 8, tg), F32),
        pltpu.VMEM((experts, tg), F32),
        pltpu.VMEM((experts, tg), F32),
        pltpu.VMEM((rows, tg), BF16),
        pltpu.VMEM((rows, tg), BF16),
        pltpu.VMEM((nrows, dc), BF16),
        pltpu.VMEM((ny, rows - nrows, dc), BF16),
        pltpu.VMEM((2, ny, rows, dc), BF16),
        pltpu.VMEM((most, 2 * f), F32),
        pltpu.VMEM((most, f), BF16),
        pltpu.VMEM((ny, rows, dc), BF16),
        pltpu.VMEM((ny, rows, dc), BF16),
        pltpu.VMEM((ny, rows, dc), BF16),
        pltpu.VMEM((nrows, dc), BF16),
        pltpu.VMEM((2, nrows, dc), BF16),
        pltpu.VMEM((nrows, dc), BF16),
        pltpu.VMEM((ny, rows - nrows, dc), BF16),
        pltpu.VMEM((3, tg, dc), BF16),
        pltpu.VMEM((3, tg, dc), BF16),
        pltpu.VMEM((tg, dc), F32),
        pltpu.VMEM((tg, dc), F32),
        pltpu.VMEM((tg, dc), BF16),
        pltpu.VMEM((nt, per, dc), BF16),
        pltpu.SemaphoreType.DMA((n_local,)),
        pltpu.SemaphoreType.DMA((n_remote,)),
        pltpu.SemaphoreType.DMA((n_remote,)),
    ]
    both = pl.pallas_call(
        functools.partial(kernel, (experts, nt, nx, nz, cap, d)),
        out_shape=jax.ShapeDtypeStruct((2, per, d), BF16),
        in_specs=[hbm, hbm, vmem, vmem, vmem, hbm, hbm, hbm],
        out_specs=vmem,
        scratch_shapes=scratch,
        compiler_params=pltpu.CompilerParams(
            collective_id=0, has_side_effects=True, vmem_limit_bytes=60 * 1024 * 1024
        ),
        cost_estimate=pl.CostEstimate(
            flops=6 * rows * d * f, bytes_accessed=6 * d * f, transcendentals=rows * f
        ),
    )(
        attn_partials.reshape(tg, d),
        resid.reshape(tg, d),
        norm_gain.reshape(1, d),
        expert_ids.transpose(0, 2, 1),
        gate_num.transpose(0, 2, 1),
        w_gate.reshape(d, f),
        w_up.reshape(d, f),
        w_down.reshape(f, d),
    )
    res, mix = both[0], both[1]
    return (res.reshape(two, per // two, d), mix.reshape(two, per // two, d))


def solution(mesh):
    placed = (
        P("tensor", None, "expert", None),
        P(None, "expert", None),
        P(),
        P(None, "expert", None),
        P(None, "expert", None),
        P("expert", None, "tensor"),
        P("expert", None, "tensor"),
        P("expert", "tensor", None),
    )
    return jax.shard_map(
        shards,
        mesh=mesh,
        in_specs=placed,
        out_specs=(P(None, ("expert", "tensor"), None), P(None, ("expert", "tensor"), None)),
        check_vma=False,
    )
```

```python
import functools
import re

import jax
import jax.numpy as jnp
from jax import lax
from jax.experimental import pallas as pl
from jax.experimental.pallas import tpu as pltpu
from jax.sharding import PartitionSpec as P

MESH = pl.DeviceIdType.MESH
BF16 = jnp.bfloat16
F32 = jnp.float32
BLOCK = 8


NORMAL = "A3B2A2A4B3A1"
DIRECT = "A0B1"
SCHEDULE = (
    "P5A0P1P4P3D5P2P6D1F5P7D4H5F1P0F4D6D3C5D2H4C6F3Q5",
    "C4D7H1F2Q6H3Q4C7D0H2C3T4Q7F0Q3C2H0T5U4T3Q2C0U5U3",
    "Q0T2C1T0Q1U2U0T1V0U1W3W0W5W4W2W1",
)


def grid_of(experts):
    return (4, experts // 4) if experts >= 4 else (1, experts)


def groups_of(nx, nz):
    def offsets(name):
        far = int(name[1])
        if far in (0, nz - far):
            both = [(dx, far) for dx in range(nx)]
            return both if name[0] == "A" else both[name[0] == "c" :: 2]
        flip = name[0] in "Bbd"
        both = [(dx, far if (dx < nx // 2) != flip else nz - far) for dx in range(nx)]
        return both if name[0] in "AB" else both[name[0] in "cd" :: 2]

    if nx == 4 and nz == 8:
        return [offsets(a + b) for a, b in zip(NORMAL[::2], NORMAL[1::2])], [
            offsets(a + b) for a, b in zip(DIRECT[::2], DIRECT[1::2])
        ]
    return [[(dx, dz) for dx in range(nx)] for dz in range(1, nz)], [offsets("A0")]


def schedule_of(normal, direct):
    if normal == len(NORMAL) // 2 and direct == len(DIRECT) // 2:
        return [(name, int(g)) for name, g in re.findall("([A-Z])([0-9])", "".join(SCHEDULE))]
    steps = [("A", 0)] + [("P", g) for g in range(normal + direct)]
    for names, groups in (("DFHCQTUW", range(normal)), ("DCQ", range(normal, normal + direct))):
        steps += [(name, g) for name in names for g in groups]
    return steps + [("V", 0)]


def kernel(
    cfg,
    attn, resid, gain, ids, nums, wg, wu, wd,
    outs,
    wgu, wdv, ap, arb, afin, rsd, hs, nall, rsend, rbuf, ssend, sbuf,
    rank, gate, sel, selw, snd, snd4, xg, acc, hid, own, sib, rb, tr, fin, back, back4, msd, mrd, mine4, mix, msend, mbuf,
    lsem, ssem, rsem, ready,
):
    experts, nt, nx, nz, cap, d = cfg
    ny = nt // 2
    dc = d // nt
    tg = attn.shape[0]
    per = tg // nt
    f = wg.shape[1]
    nb = tg // BLOCK
    sl = nb * cap

    e = lax.axis_index("expert")
    t = lax.axis_index("tensor")
    x, z = e // nz, lax.rem(e, nz)
    y, c = t // 2, lax.rem(t, 2)
    step = 1 - 2 * c
    yf = lax.rem(y + step + ny, ny)
    yb = lax.rem(y - step + ny, ny)
    yo = lax.rem(y + 2, ny)
    sibling = (e, y * 2 + 1 - c)
    ahead = (e, yf * 2 + c)
    behind = (e, yb * 2 + c)
    opposite = (e, yo * 2 + c)

    offsets, groups = [], []
    normal, direct = groups_of(nx, nz)
    n = len(normal)
    for members in normal + direct:
        groups.append((len(offsets), len(offsets) + len(members)))
        offsets.extend(members)
    kd = groups[n][0]
    rd0 = kd * sl

    def expert_at(k, sign=1):
        dx, dz = offsets[k]
        ex = lax.rem(x + (dx if sign > 0 else nx - dx), nx)
        ez = lax.rem(z + (dz if sign > 0 else nz - dz), nz)
        return ex * nz + ez

    counter = {"l": 0, "s": 0, "r": 0}
    sent = []

    def fresh(kind):
        counter[kind] += 1
        return counter[kind] - 1

    def local(src, dst):
        return pltpu.make_async_copy(src, dst, lsem.at[fresh("l")])

    def remote(src, dst, device):
        copy = pltpu.make_async_remote_copy(
            src_ref=src, dst_ref=dst, send_sem=ssem.at[fresh("s")], recv_sem=rsem.at[fresh("r")],
            device_id=device, device_id_type=MESH,
        )
        copy.start()
        sent.append(copy)
        return copy

    barrier = pltpu.get_barrier_semaphore()
    peers = 0
    for k, (dx, dz) in enumerate(offsets):
        if (dx == 0) != (dz == 0):
            pl.semaphore_signal(barrier, inc=1, device_id=(expert_at(k), t), device_id_type=MESH)
            peers += 1
    for i in range(1, nt):
        pl.semaphore_signal(barrier, inc=1, device_id=(e, lax.rem(t + i, nt)), device_id_type=MESH)
        peers += 1

    def cols(ref, j):
        return ref.at[:, pl.ds(pl.multiple_of(j * dc, dc), dc)]

    own_loads = [local(cols(attn, 2 * yy + c), ap.at[yy]) for yy in (yo, yb, yf, y)]
    own_loads.append(local(cols(resid, t), rsd))
    for copy in own_loads:
        copy.start()
    w_loads = [local(wg, wgu.at[:, pl.ds(0, f)]), local(wu, wgu.at[:, pl.ds(f, f)])]
    for j in range(nt):
        w_loads.append(local(wd.at[:, pl.ds(j * dc, dc)], wdv.at[j]))
    for copy in w_loads:
        copy.start()

    pl.semaphore_wait(barrier, peers)
    for dx in range(1, nx):
        pl.semaphore_signal(
            ready, inc=1, device_id=(lax.rem(x + dx, nx) * nz + z, t), device_id_type=MESH
        )

    a1 = [remote(cols(attn, 2 * yy + 1 - c), arb.at[yy], sibling) for yy in (yo, yf, yb, y)]

    half = tg // 2
    ri = lax.broadcasted_iota(jnp.int32, (tg, tg), 0)
    ci = lax.broadcasted_iota(jnp.int32, (tg, tg), 1)
    branch = lax.rem(ci // BLOCK, 2)
    place = branch * half + ci // (2 * BLOCK) * BLOCK + lax.rem(ci, BLOCK)
    order = jnp.where(ri == place, 1.0, 0.0).astype(BF16)

    def by_device(ref):
        return sum(
            jnp.dot(
                ref[b].astype(F32).astype(BF16),
                order[b * half : (b + 1) * half],
                preferred_element_type=F32,
            )
            for b in range(2)
        )

    names, amounts = by_device(ids), by_device(nums)
    lane = lax.broadcasted_iota(jnp.int32, (experts, tg), 0).astype(F32)
    member = jnp.zeros((experts, tg), F32)
    weight = jnp.zeros((experts, tg), F32)
    for k in range(ids.shape[1]):
        hit = names[k : k + 1, :] == lane
        member = member + jnp.where(hit, 1.0, 0.0)
        weight = weight + jnp.where(hit, amounts[k : k + 1, :] * (1.0 / 128.0), 0.0)
    lower = jnp.where((ri // BLOCK == ci // BLOCK) & (ri < ci), 1.0, 0.0).astype(BF16)
    before = jnp.dot(member.astype(BF16), lower, preferred_element_type=F32)
    rank[...] = jnp.where(member > 0.5, before, -1.0)
    gate[...] = weight
    ji = lax.broadcasted_iota(jnp.int32, (sl, tg), 0)
    bi = lax.broadcasted_iota(jnp.int32, (sl, tg), 1) // BLOCK
    jd = jnp.zeros((sl, tg), jnp.int32)
    for m in range(1, nb):
        jd = jd + jnp.where(ji >= m * cap, 1, 0)
    want = jnp.where(jd == bi, (ji - jd * cap).astype(F32), -2.0)
    for k in range(experts):
        at = pl.ds(expert_at(k), 1)
        chosen = want == rank[at, :]
        sel[k * sl : (k + 1) * sl, :] = jnp.where(chosen, 1.0, 0.0).astype(BF16)
        selw[k * sl : (k + 1) * sl, :] = jnp.where(chosen, gate[at, :], 0.0).astype(BF16)

    a2 = []
    for i, (yy, peer) in enumerate(((yo, opposite), (yb, behind), (yf, ahead))):
        own_loads[i].wait()
        a1[i].wait_recv()
        ap[yy] = ap[yy] + arb[yy]
        a2.append(remote(ap.at[yy], afin.at[i], peer))
    for copy in own_loads[3:]:
        copy.wait()
    a1[3].wait_recv()
    mine = ap[y].astype(F32) + arb[y].astype(F32) + rsd[...].astype(F32)
    for i, copy in enumerate(a2):
        copy.wait_recv()
        mine = mine + afin[i].astype(F32)
    state = jnp.concatenate(
        [
            mine[b * half + i * BLOCK : b * half + (i + 1) * BLOCK]
            for i in range(nt)
            for b in range(2)
        ],
        axis=0,
    )
    hs[...] = state

    part = jnp.sum(state * state, axis=1, keepdims=True)
    ssend[...] = jnp.transpose(jnp.broadcast_to(part, (tg, tg)))[:8]
    sums = []
    for i in range(1, nt):
        sums.append(remote(ssend, sbuf.at[t], (e, lax.rem(t + i, nt))))
    sbuf[t] = ssend[...]
    rsend[...] = state.astype(BF16)

    def to_rows(src, dst):
        copies = []
        for i in range(1, nt):
            to = lax.rem(t + i, nt)
            rows = pl.ds(pl.multiple_of(to * per, per), per)
            copies.append(remote(src.at[rows], dst.at[t], (e, to)))
        keep = local(src.at[pl.ds(pl.multiple_of(t * per, per), per)], dst.at[t])
        keep.start()
        return copies, keep

    res_rows = to_rows(rsend, rbuf)
    for copy in sums:
        copy.wait_recv()
    total = sbuf[0]
    for i in range(1, nt):
        total = total + sbuf[i]
    total = jnp.transpose(jnp.concatenate([total] * (tg // 8), axis=0))
    scale = lax.rsqrt(total * (1.0 / d) + 1e-06)
    mygain = gain[:, pl.ds(pl.multiple_of(t * dc, dc), dc)]
    for j in range(dc // tg):
        at = slice(j * tg, (j + 1) * tg)
        nall[y, :, at] = (hs[:, at] * scale * mygain[:, at]).astype(BF16)

    if nx > 1:
        pl.semaphore_wait(ready, nx - 1)
    there = [None] * experts

    spread = []

    def spread_rows(g):
        for peer in (opposite, behind, ahead):
            spread.append(remote(nall.at[y], nall.at[y], peer))

    def move(k, src, dst, device):
        if offsets[k] == (0, 0):
            copy = local(src, dst)
            copy.start()
            return copy
        return remote(src, dst, device)

    def dispatch(g):
        k0, k1 = groups[g]
        rows = slice(k0 * sl, k1 * sl)
        if g < n:
            snd[rows, :] = jnp.dot(sel[rows, :], nall[y], preferred_element_type=F32).astype(BF16)
        else:
            if g == n:
                for copy in spread:
                    copy.wait_recv()
            held = slice(k0 * sl - rd0, k1 * sl - rd0)
            for yy in range(ny):
                snd4[yy, held, :] = jnp.dot(
                    sel[rows, :], nall[yy], preferred_element_type=F32
                ).astype(BF16)
        for k in range(k0, k1):
            at = pl.ds(k * sl, sl)
            if g < n:
                there[k] = move(k, snd.at[at], xg.at[c, y, at], (expert_at(k), t))
            else:
                held = pl.ds(k * sl - rd0, sl)
                there[k] = move(k, snd4.at[:, held], xg.at[c, :, at], (expert_at(k), t))

    def arrived(k, copies):
        if offsets[k] == (0, 0):
            copies[k].wait()
        else:
            copies[k].wait_recv()

    state_of = [dict() for _ in groups]

    def span(g):
        k0, k1 = groups[g]
        return k0 * sl, (k1 - k0) * sl

    def gather_first(g):
        s = state_of[g]
        r0, rn = span(g)
        for k in range(*groups[g]):
            arrived(k, there)
        if g >= n:
            block = xg.at[c, :, pl.ds(r0, rn)]
            s["near"] = [remote(block, block, sibling)]
            return
        block = xg.at[c, y, pl.ds(r0, rn)]
        s["b"] = remote(block, block, ahead)
        s["f"] = remote(block, block, behind)
        s["near"] = [remote(block, block, sibling)]

    def gather_second(g):
        s = state_of[g]
        r0, rn = span(g)
        s["b"].wait_recv()
        block = xg.at[c, yb, pl.ds(r0, rn)]
        s["o"] = remote(block, block, ahead)
        s["near"].append(remote(block, block, sibling))
        s["f"].wait_recv()
        block = xg.at[c, yf, pl.ds(r0, rn)]
        s["near"].append(remote(block, block, sibling))

    def gather_third(g):
        s = state_of[g]
        r0, rn = span(g)
        s["o"].wait_recv()
        block = xg.at[c, yo, pl.ds(r0, rn)]
        s["near"].append(remote(block, block, sibling))

    weights_here = []

    def compute(g):
        s = state_of[g]
        r0, rn = span(g)
        for copy in s["near"]:
            copy.wait_recv()
        if not weights_here:
            weights_here.append(True)
            for copy in w_loads:
                copy.wait()
        at = pl.ds(r0, rn)
        acc[:rn, :] = jnp.zeros((rn, 2 * f), F32)

        @pl.loop(0, ny)
        def _(j):
            w = wgu[pl.ds(pl.multiple_of(j * 2 * dc, 2 * dc), 2 * dc), :]
            wide = jnp.concatenate([xg[0, j, at, :], xg[1, j, at, :]], axis=1)
            acc[:rn, :] += jnp.dot(wide, w, preferred_element_type=F32)

        a = acc[:rn, :f]
        hid[:rn, :] = (a / (1.0 + jnp.exp(-a)) * acc[:rn, f:]).astype(BF16)

        @pl.loop(0, ny)
        def _(yy):
            sib[yy, at, :] = jnp.dot(
                hid[:rn, :], wdv[yy * 2 + 1 - c], preferred_element_type=F32
            ).astype(BF16)

        s["pair"] = remote(sib.at[:, at], rb.at[:, at], sibling)

        @pl.loop(0, ny)
        def _(yy):
            own[yy, at, :] = jnp.dot(
                hid[:rn, :], wdv[yy * 2 + c], preferred_element_type=F32
            ).astype(BF16)

    back_copies = [None] * experts

    def reduce_first(g):
        s = state_of[g]
        r0, rn = span(g)
        at = pl.ds(r0, rn)
        s["pair"].wait_recv()

        def pair(i):
            own[i, at, :] = own[i, at, :] + rb[i, at, :]

        if g >= n:
            for i in range(ny):
                pair(i)
            for k in range(*groups[g]):
                here = pl.ds(k * sl, sl)
                held = pl.ds(k * sl - rd0, sl)
                back_copies[k] = move(
                    k, own.at[:, here], back4.at[:, held], (expert_at(k, -1), t)
                )
            return
        pair(yo)
        s["t"] = remote(own.at[yo, at], tr.at[at], ahead)
        pair(yb)
        s["f1"] = remote(own.at[yb, at], fin.at[1, at], behind)
        pair(yf)
        pair(y)

    def reduce_second(g):
        s = state_of[g]
        r0, rn = span(g)
        at = pl.ds(r0, rn)
        s["t"].wait_recv()
        own[yf, at, :] = own[yf, at, :] + tr[at, :]
        s["f0"] = remote(own.at[yf, at], fin.at[0, at], ahead)

    def reduce_third(g):
        s = state_of[g]
        r0, rn = span(g)
        at = pl.ds(r0, rn)
        s["f1"].wait_recv()
        s["f0"].wait_recv()
        own[y, at, :] = (
            own[y, at, :].astype(F32) + fin[0, at, :].astype(F32) + fin[1, at, :].astype(F32)
        ).astype(BF16)
        for k in range(*groups[g]):
            here = pl.ds(k * sl, sl)
            back_copies[k] = move(k, own.at[y, here], back.at[here], (expert_at(k, -1), t))

    def combine(rows, values):
        return lax.dot_general(
            selw[rows, :], values, (((0,), (0,)), ((), ())), preferred_element_type=F32
        )

    summed = []

    def combine_direct(g):
        for k in range(kd, experts):
            arrived(k, back_copies)
        rows = slice(rd0, experts * sl)
        for i, (yy, peer) in enumerate(((yo, opposite), (yb, behind), (yf, ahead))):
            msd[i] = combine(rows, back4[yy]).astype(BF16)
            summed.append(remote(msd.at[i], mrd.at[i], peer))
        mine4[...] = combine(rows, back4[y])

    mixed_groups = []

    def combine_normal(g):
        for k in range(*groups[g]):
            arrived(k, back_copies)
        r0, rn = span(g)
        rows = slice(r0, r0 + rn)
        if mixed_groups:
            mix[...] += combine(rows, back[rows, :])
        else:
            mix[...] = combine(rows, back[rows, :])
        mixed_groups.append(g)

    def to_out(copies, buf, out):
        for copy in copies[0]:
            copy.wait_recv()
        copies[1].wait()
        for j in range(nt):
            out[:, j * dc : (j + 1) * dc] = buf[j]

    def residual_out(g):
        to_out(res_rows, rbuf, outs.at[0])

    steps = dict(
        P=dispatch, D=gather_first, F=gather_second, H=gather_third, C=compute,
        Q=reduce_first, T=reduce_second, U=reduce_third, A=spread_rows, V=combine_direct,
        W=combine_normal,
    )
    for name, g in schedule_of(n, len(direct)):
        steps[name](g)
        if name == "V":
            residual_out(g)

    mixed = mine4[...] + mix[...]
    for i, copy in enumerate(summed):
        copy.wait_recv()
        mixed = mixed + mrd[i].astype(F32)
    msend[...] = mixed.astype(BF16)
    done = list(sent)
    last = to_rows(msend, mbuf)
    for copy in done:
        copy.wait_send()
    to_out(last, mbuf, outs.at[1])
    for copy in sent[len(done) :]:
        copy.wait_send()


def shards(attn_partials, resid, norm_gain, expert_ids, gate_num, w_gate, w_up, w_down):
    experts = lax.axis_size("expert")
    nt = lax.axis_size("tensor")
    nx, nz = grid_of(experts)
    _, two, tokens, d = attn_partials.shape
    top = expert_ids.shape[-1]
    tg = two * tokens
    per = tg // nt
    dc = d // nt
    ny = nt // 2
    f = w_gate.shape[-1]
    cap = min(BLOCK, 3 * BLOCK * top // (2 * experts))
    sl = tg // BLOCK * cap
    rows = experts * sl
    normal, direct = groups_of(nx, nz)
    most = max(len(g) for g in normal + direct) * sl
    nrows = sum(len(g) for g in normal) * sl
    n_groups = len(normal + direct)

    n_remote = 4 + 3 + 2 * (experts - 1) + 3 * (nt - 1) + 12 * n_groups + ny + 8
    n_local = ny + 3 + nt + 4
    vmem = pl.BlockSpec(memory_space=pltpu.VMEM)
    hbm = pl.BlockSpec(memory_space=pl.ANY)
    scratch = [
        pltpu.VMEM((d, 2 * f), BF16),
        pltpu.VMEM((nt, f, dc), BF16),
        pltpu.VMEM((ny, tg, dc), BF16),
        pltpu.VMEM((ny, tg, dc), BF16),
        pltpu.VMEM((3, tg, dc), BF16),
        pltpu.VMEM((tg, dc), BF16),
        pltpu.VMEM((tg, dc), F32),
        pltpu.VMEM((ny, tg, dc), BF16),
        pltpu.VMEM((tg, dc), BF16),
        pltpu.VMEM((nt, per, dc), BF16),
        pltpu.VMEM((8, tg), F32),
        pltpu.VMEM((nt, 8, tg), F32),
        pltpu.VMEM((experts, tg), F32),
        pltpu.VMEM((experts, tg), F32),
        pltpu.VMEM((rows, tg), BF16),
        pltpu.VMEM((rows, tg), BF16),
        pltpu.VMEM((nrows, dc), BF16),
        pltpu.VMEM((ny, rows - nrows, dc), BF16),
        pltpu.VMEM((2, ny, rows, dc), BF16),
        pltpu.VMEM((most, 2 * f), F32),
        pltpu.VMEM((most, f), BF16),
        pltpu.VMEM((ny, rows, dc), BF16),
        pltpu.VMEM((ny, rows, dc), BF16),
        pltpu.VMEM((ny, rows, dc), BF16),
        pltpu.VMEM((nrows, dc), BF16),
        pltpu.VMEM((2, nrows, dc), BF16),
        pltpu.VMEM((nrows, dc), BF16),
        pltpu.VMEM((ny, rows - nrows, dc), BF16),
        pltpu.VMEM((3, tg, dc), BF16),
        pltpu.VMEM((3, tg, dc), BF16),
        pltpu.VMEM((tg, dc), F32),
        pltpu.VMEM((tg, dc), F32),
        pltpu.VMEM((tg, dc), BF16),
        pltpu.VMEM((nt, per, dc), BF16),
        pltpu.SemaphoreType.DMA((n_local,)),
        pltpu.SemaphoreType.DMA((n_remote,)),
        pltpu.SemaphoreType.DMA((n_remote,)),
        pltpu.SemaphoreType.REGULAR,
    ]
    both = pl.pallas_call(
        functools.partial(kernel, (experts, nt, nx, nz, cap, d)),
        out_shape=jax.ShapeDtypeStruct((2, per, d), BF16),
        in_specs=[hbm, hbm, vmem, vmem, vmem, hbm, hbm, hbm],
        out_specs=vmem,
        scratch_shapes=scratch,
        compiler_params=pltpu.CompilerParams(
            collective_id=0, has_side_effects=True, vmem_limit_bytes=60 * 1024 * 1024
        ),
        cost_estimate=pl.CostEstimate(
            flops=6 * rows * d * f, bytes_accessed=6 * d * f, transcendentals=rows * f
        ),
    )(
        attn_partials.reshape(tg, d),
        resid.reshape(tg, d),
        norm_gain.reshape(1, d),
        expert_ids.transpose(0, 2, 1),
        gate_num.transpose(0, 2, 1),
        w_gate.reshape(d, f),
        w_up.reshape(d, f),
        w_down.reshape(f, d),
    )
    res, mix = both[0], both[1]
    return (res.reshape(two, per // two, d), mix.reshape(two, per // two, d))


def solution(mesh):
    placed = (
        P("tensor", None, "expert", None),
        P(None, "expert", None),
        P(),
        P(None, "expert", None),
        P(None, "expert", None),
        P("expert", None, "tensor"),
        P("expert", None, "tensor"),
        P("expert", "tensor", None),
    )
    return jax.shard_map(
        shards,
        mesh=mesh,
        in_specs=placed,
        out_specs=(P(None, ("expert", "tensor"), None), P(None, ("expert", "tensor"), None)),
        check_vma=False,
    )
```
